32 devices in a mesh: col: 16 (over z, x, core), row: 2 (over y).
Axes of the slice: x: 2, y: 2, z: 4, core: 2. Of those that a mesh axis runs over, the one named last changes fastest.
Arguments:
- weight: bfloat16 [8192, 53248], P('row', 'col'), may hold values from -6 to 6
- factor: float32 [1664, 53248], P('row', 'col'), may hold values from -1 to 2, as said below
- keep_mask: int32 [64, 13], P('row'), may hold values 0 or 1
Outputs:
- pruned: bfloat16 [8192, 53248], P('row', 'col')
The draws below stay inside these ranges and needn't reach their ends.
Inputs may be any that keep to these rules, and one draw needn't show every extreme that they name: factor[i, k] = 0 for k < i; the diagonal entries factor[i, i] lie in [0.5, 2].
All inputs are finite; a program needn't handle non-finite values. No bound on the sum of `keep_mask` on one device may be relied on, other than what follows from the above.
Results may differ from the reference program's by a relative error of at most 0.0035.
Values may be sent and summed in bfloat16 or wider, within the bound.
A program may use at most 320 MiB of HBM per device.

```python
import math
import jax
import jax.numpy as jnp
from jax import lax

ROWS = 8192
COLS = 53248
BLK = 128
PCOLS = 1664


def draw_factor(key, part):
    key_noise, key_pivot = jax.random.split(jax.random.fold_in(key, 7), 2)
    noise_draw = jnp.clip(jax.random.normal(key_noise, (PCOLS, COLS), jnp.float32), -6.0, 6.0)
    off_values = 0.4 * noise_draw / math.sqrt(PCOLS)
    pivot_values = jnp.exp(jax.random.uniform(key_pivot, (PCOLS, 1), jnp.float32, math.log(0.5), math.log(2.0)))
    row_ids = jnp.arange(PCOLS, dtype=jnp.int32)[:, None]
    col_ids = jnp.arange(COLS, dtype=jnp.int32)[None, :]
    factor_out = jnp.where(col_ids > row_ids, off_values, jnp.where(col_ids == row_ids, pivot_values, 0.0))
    return factor_out.astype(jnp.float32)


def set_ends(values, rng, smallest, largest):
    longest = values.shape.index(max(values.shape))
    spots = []
    for shift in (0, 1):
        where = [jax.random.randint(jax.random.fold_in(rng, axis), (), 0, length) for axis, length in enumerate(values.shape)]
        where[longest] = (where[longest] + shift) % values.shape[longest]
        spots.append(tuple(where))
    return values.at[spots[0]].set(smallest).at[spots[1]].set(largest)


def shard_levels(key, dims, cuts, least, top_value):
    def one(axis_at, blocks):
        draws = jax.random.uniform(jax.random.fold_in(jax.random.fold_in(key, 6), axis_at), (blocks,), jnp.float32, least / len(cuts), top_value / len(cuts))
        return jnp.repeat(jnp.exp(draws), dims[axis_at] // blocks).reshape((-1,) + (1,) * (len(dims) - axis_at - 1))

    loudness = one(*cuts[0])
    for cut in cuts[1:]:
        loudness = loudness * one(*cut)
    return loudness


def centred(key, shape, width, reach, pieces=(), held_as=jnp.bfloat16):
    array = width * jax.random.normal(key, shape, jnp.float32)
    if pieces:
        array = array * shard_levels(key, shape, pieces, -0.22, 0.18)
    return jnp.clip(array, -reach, reach).astype(held_as)


def setup_inputs(seed: int = 0) -> dict:
    arg_keys = jax.random.split(jax.random.key(seed), 4)
    return {
        "weight": centred(arg_keys[0], (ROWS, COLS), 1.0, 6.0, ((0, 2), (1, 16))),
        "factor": draw_factor(jax.random.fold_in(arg_keys[3], 71), 0),
        "keep_mask": set_ends((jax.random.randint(arg_keys[2], (ROWS // BLK, PCOLS // BLK), 0, 2) < 1).astype(jnp.int32), jax.random.fold_in(arg_keys[2], 1), 0, 1),
    }


def prune_block(block_weight, block_keep, block_factor):
    block_width = block_weight.shape[1]
    positions = jnp.arange(block_width, dtype=jnp.int32)

    def advance(column_at, carried):
        current, errors = carried
        column_at = jnp.asarray(column_at).astype(jnp.int32)
        column = lax.dynamic_slice_in_dim(current, column_at, 1, 1)
        keep_col = lax.dynamic_slice_in_dim(block_keep, column_at, 1, 1)
        factor_row = lax.dynamic_slice_in_dim(block_factor, column_at, 1, 0)
        pivot_value = jnp.sum(jnp.where(positions == column_at, factor_row[0], jnp.float32(0.0)))
        error_col = column * (1.0 - keep_col) / pivot_value
        later_mask = (positions > column_at)[None, :]
        current = current - jnp.where(later_mask, error_col * factor_row, jnp.float32(0.0))
        errors = errors + jnp.where((positions == column_at)[None, :], error_col, jnp.float32(0.0))
        return current, errors

    current, errors = lax.fori_loop(0, block_width, advance, (block_weight, jnp.zeros_like(block_weight)))
    return current * block_keep, errors


def reference(weight, factor, keep_mask):
    panel_w = weight[:, :PCOLS].astype(jnp.float32)
    keep_full = jnp.repeat(jnp.repeat(keep_mask.astype(jnp.float32), BLK, axis=0), BLK, axis=1)
    diag_block = factor[:, :PCOLS]
    kept_parts = []
    error_parts = []
    for block_id in range(PCOLS // BLK):
        low_col = block_id * BLK
        high_col = low_col + BLK
        kept_part, error_part = prune_block(panel_w[:, low_col:high_col], keep_full[:, low_col:high_col], diag_block[low_col:high_col, low_col:high_col])
        kept_parts.append(kept_part)
        error_parts.append(error_part)
        update = jnp.dot(error_part, diag_block[low_col:high_col, high_col:], precision=lax.Precision.HIGHEST)
        panel_w = jnp.concatenate([panel_w[:, :high_col], panel_w[:, high_col:] - update], axis=1)
    kept = jnp.concatenate(kept_parts, axis=1).astype(jnp.bfloat16)
    errors = jnp.concatenate(error_parts, axis=1)
    errors_low = lax.optimization_barrier(errors.astype(jnp.bfloat16)).astype(jnp.float32)
    rest_blocks = COLS // PCOLS - 1
    rest_weight = weight[:, PCOLS:].reshape(ROWS, rest_blocks, PCOLS).transpose(1, 0, 2)
    rest_factor = factor[:, PCOLS:].reshape(PCOLS, rest_blocks, PCOLS).transpose(1, 0, 2)

    def compensate(pair):
        block_weight, block_factor = pair
        factor_low = lax.optimization_barrier(block_factor.astype(jnp.bfloat16)).astype(jnp.float32)
        product = jnp.dot(errors_low, factor_low, precision=lax.Precision.HIGHEST)
        return (block_weight.astype(jnp.float32) - product).astype(jnp.bfloat16)

    rest_out = lax.map(compensate, (rest_weight, rest_factor))
    rest_out = rest_out.transpose(1, 0, 2).reshape(ROWS, COLS - PCOLS)
    return jnp.concatenate([kept, rest_out], axis=1)
```

```python
from functools import partial

import jax
import jax.numpy as jnp
from jax import lax
from jax.experimental import pallas as pl
from jax.experimental.pallas import tpu as pltpu
from jax.sharding import PartitionSpec as P

BLK = 128
SUP = 256
VMEM_BYTES = 60 * 1024 * 1024


def split(x):
    high = x.astype(jnp.bfloat16)
    low = (x - high.astype(jnp.float32)).astype(jnp.bfloat16)
    return high, low


def mul(a, b):
    return jnp.dot(a, b, preferred_element_type=jnp.float32)


def mul3(a, b):
    a_high, a_low = split(a)
    b_high, b_low = split(b)
    return mul(a_high, b_high) + (mul(a_high, b_low) + mul(a_low, b_high))


def prune_kernel(
    keep_ref, w_ref, f_ref, e_ref, kept_ref, f_high, f_low, blocks, inv, inv_high, inv_low, e_low
):
    chunk, pcols = w_ref.shape
    supers = inv.shape[0]
    row_id = lax.broadcasted_iota(jnp.int32, (SUP, SUP), 0)
    col_id = lax.broadcasted_iota(jnp.int32, (SUP, SUP), 1)

    @pl.when(pl.program_id(0) == 0)
    def _():
        for low in range(0, pcols, BLK):
            rows = slice(low, low + BLK)
            high_part, low_part = split(f_ref[rows, :])
            f_high[rows, :] = high_part
            f_low[rows, :] = low_part
        eye = row_id == col_id
        pair = (row_id // 2 == col_id // 2) & (row_id < col_id)
        for s in range(supers):
            lo = s * SUP
            width = min(SUP, pcols - lo)
            if width < SUP:
                blocks[s] = jnp.where(eye, 1.0, 0.0)
            blocks[s, :width, :width] = f_ref[lo : lo + width, lo : lo + width]
            block = blocks[s]
            diagonal = jnp.where(eye, block, 0.0)
            per_row = 1.0 / jnp.sum(diagonal, axis=1, keepdims=True)
            per_col = 1.0 / jnp.sum(diagonal, axis=0, keepdims=True)
            inv[s] = jnp.where(
                eye, per_row, jnp.where(pair, -(block * per_row) * per_col, 0.0)
            )

        def level(bit, carry):
            mask = (
                ((row_id >> (bit + 1)) == (col_id >> (bit + 1)))
                & (((row_id >> bit) & 1) == 0)
                & (((col_id >> bit) & 1) == 1)
            )
            for s in range(supers):
                x = inv[s]
                inv[s] = x - mul3(mul3(x, jnp.where(mask, blocks[s], 0.0)), x)
            return carry

        lax.fori_loop(1, SUP.bit_length() - 1, level, 0)
        for s in range(supers):
            high_part, low_part = split(inv[s])
            inv_high[s] = high_part
            inv_low[s] = low_part

    row_blocks = chunk // BLK
    base = pl.program_id(0) * row_blocks
    for s in range(supers):
        lo = s * SUP
        width = min(SUP, pcols - lo)
        cols = slice(lo, lo + width)
        current = w_ref[:, cols].astype(jnp.float32)
        if lo:
            head = e_ref[:, :lo]
            current = current - (
                mul(head, f_high[:lo, cols])
                + (mul(head, f_low[:lo, cols]) + mul(e_low[:, :lo], f_high[:lo, cols]))
            )
        drop_rows = []
        for g in range(row_blocks):
            parts = []
            for b in range(lo // BLK, (lo + width) // BLK):
                kept_here = keep_ref[base + g, b].astype(jnp.float32)
                parts.append(jnp.full((BLK, BLK), 1.0 - kept_here, jnp.float32))
            drop_rows.append(parts[0] if len(parts) == 1 else jnp.concatenate(parts, axis=1))
        drop = jnp.concatenate(drop_rows, axis=0)
        c_high, c_low = split(jnp.where(drop > 0.5, current, 0.0))
        i_high = inv_high[s, :width, :width]
        solved = mul(c_high, i_high) + (
            mul(c_high, inv_low[s, :width, :width]) + mul(c_low, i_high)
        )
        high_part, low_part = split(jnp.where(drop > 0.5, solved, 0.0))
        e_ref[:, cols] = high_part
        e_low[:, cols] = low_part
        first = slice(lo, lo + BLK)
        kept_ref[:, first] = jnp.where(drop[:, :BLK] > 0.5, 0.0, current[:, :BLK]).astype(
            jnp.bfloat16
        )
        if width > BLK:
            second = slice(lo + BLK, lo + width)
            c_high, c_low = high_part[:, :BLK], low_part[:, :BLK]
            inner = mul(c_high, f_high[first, second]) + (
                mul(c_high, f_low[first, second]) + mul(c_low, f_high[first, second])
            )
            kept_ref[:, second] = jnp.where(
                drop[:, BLK:] > 0.5, 0.0, current[:, BLK:] - inner
            ).astype(jnp.bfloat16)


def prune(panel, diag, keep_rows):
    rows, pcols = panel.shape
    chunk = min(rows, 512)
    supers = pl.cdiv(pcols, SUP)
    row_spec = pl.BlockSpec((chunk, pcols), lambda i: (i, 0))
    out = jax.ShapeDtypeStruct((rows, pcols), jnp.bfloat16)
    return pl.pallas_call(
        prune_kernel,
        grid=(rows // chunk,),
        out_shape=(out, out),
        in_specs=[
            pl.BlockSpec(memory_space=pltpu.SMEM),
            row_spec,
            pl.BlockSpec((pcols, pcols), lambda i: (0, 0), pipeline_mode=pl.Buffered(1)),
        ],
        out_specs=(row_spec, row_spec),
        scratch_shapes=[
            pltpu.VMEM((pcols, pcols), jnp.bfloat16),
            pltpu.VMEM((pcols, pcols), jnp.bfloat16),
            pltpu.VMEM((supers, SUP, SUP), jnp.float32),
            pltpu.VMEM((supers, SUP, SUP), jnp.float32),
            pltpu.VMEM((supers, SUP, SUP), jnp.bfloat16),
            pltpu.VMEM((supers, SUP, SUP), jnp.bfloat16),
            pltpu.VMEM((chunk, pcols), jnp.bfloat16),
        ],
        compiler_params=pltpu.CompilerParams(vmem_limit_bytes=VMEM_BYTES),
        cost_estimate=pl.CostEstimate(
            flops=6 * rows * pcols * pcols,
            bytes_accessed=6 * rows * pcols + 4 * pcols * pcols,
            transcendentals=0,
        ),
        name="prune_panel",
    )(keep_rows, panel, diag)


def spread_kernel(chips, pieces, mine_ref, all_ref, local_sem, out_send, out_recv, sib_send, sib_recv):
    index = lax.axis_index("col")
    core = index % 2
    chip = index // 2
    odd = chip % 2
    place = odd * ((chip + 1) // 2) + (1 - odd) * ((chips - chip // 2) % chips)

    def chip_at(p):
        upper = (p + chips // 2 - 1) // chips
        return (1 - upper) * (2 * p - 1) + upper * (2 * (chips - p)) + (chips - p) // chips

    step = (1 - core) * place + core * ((chips - place) % chips)
    way = 1 - 2 * core
    after = chip_at((place + way + chips) % chips) * 2 + core
    before = chip_at((place - way + chips) % chips) * 2 + core
    sibling = chip * 2 + 1 - core
    half = mine_ref.shape[0]
    size = half // pieces

    def signal(where, sem):
        pl.semaphore_signal(sem, inc=1, device_id={"col": where}, device_id_type=pl.DeviceIdType.MESH)

    barrier = pltpu.get_barrier_semaphore()
    signal(sibling, barrier)

    @pl.when(step > 0)
    def _():
        signal(before, barrier)

    @pl.when(step < chips - 1)
    def _():
        pl.semaphore_wait(barrier, 2)

    @pl.when(step == chips - 1)
    def _():
        pl.semaphore_wait(barrier, 1)

    def piece(which, t):
        return all_ref.at[pl.ds(pl.multiple_of(which * half + t * size, 16), size)]

    def forward(t):
        return pltpu.make_async_remote_copy(
            src_ref=piece(core, t),
            dst_ref=piece(core, t),
            send_sem=out_send.at[t],
            recv_sem=out_recv.at[t],
            device_id={"col": after},
            device_id_type=pl.DeviceIdType.MESH,
        )

    def across(t, which):
        return pltpu.make_async_remote_copy(
            src_ref=piece(which, t),
            dst_ref=piece(which, t),
            send_sem=sib_send.at[t],
            recv_sem=sib_recv.at[t],
            device_id={"col": sibling},
            device_id_type=pl.DeviceIdType.MESH,
        )

    @pl.when(step == 0)
    def _():
        copy = pltpu.make_async_copy(
            mine_ref, all_ref.at[pl.ds(pl.multiple_of(core * half, 16), half)], local_sem
        )
        copy.start()
        copy.wait()

    def pass_on(t, carry):
        @pl.when(step > 0)
        def _():
            forward(t).wait_recv()

        @pl.when(step < chips - 1)
        def _():
            forward(t).start()

        across(t, core).start()
        return carry

    lax.fori_loop(0, pieces, pass_on, 0)

    def finish(t, carry):
        @pl.when(step < chips - 1)
        def _():
            forward(t).wait_send()

        across(t, core).wait_send()
        across(t, 1 - core).wait_recv()
        return carry

    lax.fori_loop(0, pieces, finish, 0)


def spread(errors, devices):
    half, pcols = errors.shape
    pieces = half // 64
    return pl.pallas_call(
        partial(spread_kernel, devices // 2, pieces),
        out_shape=jax.ShapeDtypeStruct((2 * half, pcols), jnp.bfloat16),
        in_specs=[pl.BlockSpec(memory_space=pl.ANY)],
        out_specs=pl.BlockSpec(memory_space=pl.ANY),
        scratch_shapes=[pltpu.SemaphoreType.DMA] + [pltpu.SemaphoreType.DMA((pieces,))] * 4,
        compiler_params=pltpu.CompilerParams(collective_id=0, has_side_effects=True),
        cost_estimate=pl.CostEstimate(
            flops=0, bytes_accessed=16 * half * pcols, transcendentals=0
        ),
        name="spread_errors",
    )(errors)


def trail_kernel(owner_ref, e_ref, f_ref, w_ref, kept_ref, out_ref):
    pcols = e_ref.shape[1]
    width = w_ref.shape[1]
    owner = owner_ref[0] == 1

    def compensated(cols):
        product = mul(e_ref[...], f_ref[:, cols])
        return (w_ref[:, cols].astype(jnp.float32) - product).astype(jnp.bfloat16)

    @pl.when(owner)
    def _():
        out_ref[:, :pcols] = kept_ref[...]

    @pl.when(jnp.logical_not(owner))
    def _():
        for low in range(0, pcols, SUP):
            cols = slice(low, min(low + SUP, pcols))
            out_ref[:, cols] = compensated(cols)

    for low in range(pcols, width, SUP):
        cols = slice(low, min(low + SUP, width))
        out_ref[:, cols] = compensated(cols)


def trail(owner, errors, factor_low, weight, kept):
    rows, width = weight.shape
    pcols = errors.shape[1]
    tile = min(rows, 512)
    return pl.pallas_call(
        trail_kernel,
        grid=(rows // tile,),
        out_shape=jax.ShapeDtypeStruct(weight.shape, weight.dtype),
        in_specs=[
            pl.BlockSpec(memory_space=pltpu.SMEM),
            pl.BlockSpec((tile, pcols), lambda i: (i, 0)),
            pl.BlockSpec((pcols, width), lambda i: (0, 0), pipeline_mode=pl.Buffered(1)),
            pl.BlockSpec((tile, width), lambda i: (i, 0)),
            pl.BlockSpec((tile, pcols), lambda i: (i, 0)),
        ],
        out_specs=pl.BlockSpec((tile, width), lambda i: (i, 0)),
        compiler_params=pltpu.CompilerParams(vmem_limit_bytes=VMEM_BYTES),
        cost_estimate=pl.CostEstimate(
            flops=2 * rows * pcols * width,
            bytes_accessed=4 * rows * width + 2 * pcols * width,
            transcendentals=0,
        ),
        name="compensate_later",
    )(owner, errors, factor_low, weight, kept)


def per_device(weight, factor, keep_mask, *, cols_n, rows_n):
    section = lax.axis_index("col")
    lane = lax.axis_index("row")
    depth = factor.shape[0]
    pcols = depth * rows_n
    rows = weight.shape[0]
    half = rows // 2
    to_core = [(r, rows_n + r) for r in range(rows_n)]

    def move(x, pairs):
        return lax.ppermute(x, ("col", "row"), pairs)

    own = factor[:, :pcols]
    panel = weight[:, :pcols]
    received = [own] + [
        move(own, [(r, (r + s) % rows_n) for r in range(rows_n)]) for s in range(1, rows_n)
    ]
    far_panel = move(panel[half:], to_core)
    second = section == 1
    pieces = [jnp.where(second, move(x, to_core), x) for x in received]
    stacked = jnp.concatenate(pieces, axis=0)
    if rows_n > 1:
        order = jnp.stack(pieces, axis=0)
        stacked = jnp.concatenate(
            [
                lax.dynamic_index_in_dim(order, (lane - g) % rows_n, 0, keepdims=False)
                for g in range(rows_n)
            ],
            axis=0,
        )
    near_keep, far_keep = jnp.split(keep_mask, 2, axis=0)
    keep_rows = jnp.where(second, far_keep, near_keep)
    my_panel = jnp.where(second, far_panel, panel[:half])

    factor_in, _ = lax.optimization_barrier((factor, received[-1]))
    factor_low = lax.all_gather(factor_in.astype(jnp.bfloat16), "row", axis=0, tiled=True)

    def blank(panel_part, diag, keep_part):
        zeros = jnp.zeros(panel_part.shape, jnp.bfloat16)
        return zeros, zeros

    errors, kept = lax.cond(section < 2, prune, blank, my_panel, stacked, keep_rows)
    far_kept = move(kept, [(rows_n + r, r) for r in range(rows_n)])
    arrived = spread(errors, cols_n)
    kept_all = jnp.concatenate([kept, far_kept], axis=0)
    owner = (section == 0).astype(jnp.int32).reshape(1)
    return trail(owner, arrived, factor_low, weight, kept_all)


def solution(mesh):
    in_specs = (P("row", "col"), P("row", "col"), P("row", None))
    out_specs = P("row", "col")
    return jax.shard_map(
        partial(per_device, cols_n=mesh.shape["col"], rows_n=mesh.shape["row"]),
        mesh=mesh,
        in_specs=in_specs,
        out_specs=out_specs,
        check_vma=False,
    )
```

```python
from functools import partial

import jax
import jax.numpy as jnp
from jax import lax
from jax.experimental import pallas as pl
from jax.experimental.pallas import tpu as pltpu
from jax.sharding import PartitionSpec as P

BLK = 128
SUP = 256
VMEM_BYTES = 60 * 1024 * 1024


def split(x):
    high = x.astype(jnp.bfloat16)
    low = (x - high.astype(jnp.float32)).astype(jnp.bfloat16)
    return high, low


def mul(a, b):
    return jnp.dot(a, b, preferred_element_type=jnp.float32)


def mul3(a, b):
    a_high, a_low = split(a)
    b_high, b_low = split(b)
    return mul(a_high, b_high) + (mul(a_high, b_low) + mul(a_low, b_high))


def prune_kernel(lanes, lane_ref, keep_ref, w_ref, *refs):
    pieces = refs[:lanes]
    e_ref, kept_ref, f_ref, f_high, f_low, blocks, inv, inv_high, inv_low, e_low, sems = refs[lanes:]
    chunk, pcols = w_ref.shape
    depth = pcols // lanes
    supers = inv.shape[0]
    row_id = lax.broadcasted_iota(jnp.int32, (SUP, SUP), 0)
    col_id = lax.broadcasted_iota(jnp.int32, (SUP, SUP), 1)

    @pl.when(pl.program_id(0) == 0)
    def _():
        copies = []
        for s in range(lanes):
            place = lax.rem(lane_ref[0] + lanes - s, lanes)
            copies.append(
                pltpu.make_async_copy(
                    pieces[s],
                    f_ref.at[pl.ds(pl.multiple_of(place * depth, 8), depth)],
                    sems.at[s],
                )
            )
        for copy in copies:
            copy.start()
        for copy in copies:
            copy.wait()
        for low in range(0, pcols, BLK):
            rows = slice(low, low + BLK)
            high_part, low_part = split(f_ref[rows, :])
            f_high[rows, :] = high_part
            f_low[rows, :] = low_part
        eye = row_id == col_id
        pair = (row_id // 2 == col_id // 2) & (row_id < col_id)
        for s in range(supers):
            lo = s * SUP
            width = min(SUP, pcols - lo)
            if width < SUP:
                blocks[s] = jnp.where(eye, 1.0, 0.0)
            blocks[s, :width, :width] = f_ref[lo : lo + width, lo : lo + width]
            block = blocks[s]
            diagonal = jnp.where(eye, block, 0.0)
            per_row = 1.0 / jnp.sum(diagonal, axis=1, keepdims=True)
            per_col = 1.0 / jnp.sum(diagonal, axis=0, keepdims=True)
            inv[s] = jnp.where(
                eye, per_row, jnp.where(pair, -(block * per_row) * per_col, 0.0)
            )

        def level(bit, carry):
            mask = (
                ((row_id >> (bit + 1)) == (col_id >> (bit + 1)))
                & (((row_id >> bit) & 1) == 0)
                & (((col_id >> bit) & 1) == 1)
            )
            for s in range(supers):
                x = inv[s]
                inv[s] = x - mul3(mul3(x, jnp.where(mask, blocks[s], 0.0)), x)
            return carry

        lax.fori_loop(1, SUP.bit_length() - 1, level, 0)
        for s in range(supers):
            high_part, low_part = split(inv[s])
            inv_high[s] = high_part
            inv_low[s] = low_part

    row_blocks = chunk // BLK
    base = pl.program_id(0) * row_blocks
    for s in range(supers):
        lo = s * SUP
        width = min(SUP, pcols - lo)
        cols = slice(lo, lo + width)
        current = w_ref[:, cols].astype(jnp.float32)
        if lo:
            head = e_ref[:, :lo]
            current = current - (
                mul(head, f_high[:lo, cols])
                + (mul(head, f_low[:lo, cols]) + mul(e_low[:, :lo], f_high[:lo, cols]))
            )
        drop_rows = []
        for g in range(row_blocks):
            parts = []
            for b in range(lo // BLK, (lo + width) // BLK):
                kept_here = keep_ref[base + g, b].astype(jnp.float32)
                parts.append(jnp.full((BLK, BLK), 1.0 - kept_here, jnp.float32))
            drop_rows.append(parts[0] if len(parts) == 1 else jnp.concatenate(parts, axis=1))
        drop = jnp.concatenate(drop_rows, axis=0)
        c_high, c_low = split(jnp.where(drop > 0.5, current, 0.0))
        i_high = inv_high[s, :width, :width]
        solved = mul(c_high, i_high) + (
            mul(c_high, inv_low[s, :width, :width]) + mul(c_low, i_high)
        )
        high_part, low_part = split(jnp.where(drop > 0.5, solved, 0.0))
        e_ref[:, cols] = high_part
        e_low[:, cols] = low_part
        first = slice(lo, lo + BLK)
        kept_ref[:, first] = jnp.where(drop[:, :BLK] > 0.5, 0.0, current[:, :BLK]).astype(
            jnp.bfloat16
        )
        if width > BLK:
            second = slice(lo + BLK, lo + width)
            c_high, c_low = high_part[:, :BLK], low_part[:, :BLK]
            inner = mul(c_high, f_high[first, second]) + (
                mul(c_high, f_low[first, second]) + mul(c_low, f_high[first, second])
            )
            kept_ref[:, second] = jnp.where(
                drop[:, BLK:] > 0.5, 0.0, current[:, BLK:] - inner
            ).astype(jnp.bfloat16)


def prune(lane, panel, keep_rows, *pieces):
    rows, pcols = panel.shape
    chunk = min(rows, 512)
    supers = pl.cdiv(pcols, SUP)
    lanes = len(pieces)
    row_spec = pl.BlockSpec((chunk, pcols), lambda i: (i, 0))
    out = jax.ShapeDtypeStruct((rows, pcols), jnp.bfloat16)
    return pl.pallas_call(
        partial(prune_kernel, lanes),
        grid=(rows // chunk,),
        out_shape=(out, out),
        in_specs=[
            pl.BlockSpec(memory_space=pltpu.SMEM),
            pl.BlockSpec(memory_space=pltpu.SMEM),
            row_spec,
        ]
        + [pl.BlockSpec(memory_space=pl.ANY)] * lanes,
        out_specs=(row_spec, row_spec),
        scratch_shapes=[
            pltpu.VMEM((pcols, pcols), jnp.float32),
            pltpu.VMEM((pcols, pcols), jnp.bfloat16),
            pltpu.VMEM((pcols, pcols), jnp.bfloat16),
            pltpu.VMEM((supers, SUP, SUP), jnp.float32),
            pltpu.VMEM((supers, SUP, SUP), jnp.float32),
            pltpu.VMEM((supers, SUP, SUP), jnp.bfloat16),
            pltpu.VMEM((supers, SUP, SUP), jnp.bfloat16),
            pltpu.VMEM((chunk, pcols), jnp.bfloat16),
            pltpu.SemaphoreType.DMA((lanes,)),
        ],
        compiler_params=pltpu.CompilerParams(vmem_limit_bytes=VMEM_BYTES),
        cost_estimate=pl.CostEstimate(
            flops=6 * rows * pcols * pcols,
            bytes_accessed=6 * rows * pcols + 4 * pcols * pcols,
            transcendentals=0,
        ),
        name="prune_panel",
    )(lane, keep_rows, panel, *pieces)


def spread_kernel(chips, pieces, mine_ref, all_ref, out_send, out_recv, sib_send, sib_recv):
    index = lax.axis_index("col")
    core = index % 2
    chip = index // 2
    odd = chip % 2
    place = odd * ((chip + 1) // 2) + (1 - odd) * ((chips - chip // 2) % chips)

    def chip_at(p):
        upper = (p + chips // 2 - 1) // chips
        return (1 - upper) * (2 * p - 1) + upper * (2 * (chips - p)) + (chips - p) // chips

    step = (1 - core) * place + core * ((chips - place) % chips)
    way = 1 - 2 * core
    after = chip_at((place + way + chips) % chips) * 2 + core
    before = chip_at((place - way + chips) % chips) * 2 + core
    sibling = chip * 2 + 1 - core
    half = mine_ref.shape[0]
    size = half // pieces

    def signal(where, sem):
        pl.semaphore_signal(sem, inc=1, device_id={"col": where}, device_id_type=pl.DeviceIdType.MESH)

    barrier = pltpu.get_barrier_semaphore()
    signal(sibling, barrier)

    @pl.when(step > 0)
    def _():
        signal(before, barrier)

    @pl.when(step < chips - 1)
    def _():
        pl.semaphore_wait(barrier, 2)

    @pl.when(step == chips - 1)
    def _():
        pl.semaphore_wait(barrier, 1)

    def piece(which, t):
        return all_ref.at[pl.ds(pl.multiple_of(which * half + t * size, 16), size)]

    def forward(t):
        return pltpu.make_async_remote_copy(
            src_ref=piece(core, t),
            dst_ref=piece(core, t),
            send_sem=out_send.at[t],
            recv_sem=out_recv.at[t],
            device_id={"col": after},
            device_id_type=pl.DeviceIdType.MESH,
        )

    def across(t, which):
        return pltpu.make_async_remote_copy(
            src_ref=piece(which, t),
            dst_ref=piece(which, t),
            send_sem=sib_send.at[t],
            recv_sem=sib_recv.at[t],
            device_id={"col": sibling},
            device_id_type=pl.DeviceIdType.MESH,
        )

    def pass_on(t, carry):
        @pl.when(step == 0)
        def _():
            here = pl.ds(pl.multiple_of(core * half + t * size, 16), size)
            all_ref[here] = mine_ref[pl.ds(pl.multiple_of(t * size, 16), size)]

        @pl.when(step > 0)
        def _():
            forward(t).wait_recv()

        @pl.when(step < chips - 1)
        def _():
            forward(t).start()

        across(t, core).start()
        return carry

    lax.fori_loop(0, pieces, pass_on, 0)

    def finish(t, carry):
        @pl.when(step < chips - 1)
        def _():
            forward(t).wait_send()

        across(t, core).wait_send()
        across(t, 1 - core).wait_recv()
        return carry

    lax.fori_loop(0, pieces, finish, 0)


def spread(errors, devices):
    half, pcols = errors.shape
    pieces = half // 64
    return pl.pallas_call(
        partial(spread_kernel, devices // 2, pieces),
        out_shape=jax.ShapeDtypeStruct((2 * half, pcols), jnp.bfloat16),
        in_specs=[pl.BlockSpec(memory_space=pltpu.VMEM)],
        out_specs=pl.BlockSpec(memory_space=pltpu.VMEM),
        scratch_shapes=[pltpu.SemaphoreType.DMA((pieces,))] * 4,
        compiler_params=pltpu.CompilerParams(
            collective_id=0, has_side_effects=True, vmem_limit_bytes=VMEM_BYTES
        ),
        cost_estimate=pl.CostEstimate(
            flops=0, bytes_accessed=16 * half * pcols, transcendentals=0
        ),
        name="spread_errors",
    )(errors)


def trail_kernel(owner_ref, e_ref, f_ref, w_ref, near_ref, far_ref, out_ref):
    pcols = e_ref.shape[1]
    width = w_ref.shape[1]
    owner = owner_ref[0] == 1

    def compensated(cols):
        product = mul(e_ref[...], f_ref[:, cols])
        return (w_ref[:, cols].astype(jnp.float32) - product).astype(jnp.bfloat16)

    first = pl.program_id(0) < pl.num_programs(0) // 2

    @pl.when(owner & first)
    def _():
        out_ref[:, :pcols] = near_ref[...]

    @pl.when(owner & jnp.logical_not(first))
    def _():
        out_ref[:, :pcols] = far_ref[...]

    @pl.when(jnp.logical_not(owner))
    def _():
        for low in range(0, pcols, SUP):
            cols = slice(low, min(low + SUP, pcols))
            out_ref[:, cols] = compensated(cols)

    for low in range(pcols, width, SUP):
        cols = slice(low, min(low + SUP, width))
        out_ref[:, cols] = compensated(cols)


def trail(owner, errors, factor_low, weight, near, far):
    rows, width = weight.shape
    pcols = errors.shape[1]
    tile = min(rows // 2, 512)
    split_at = rows // 2 // tile
    return pl.pallas_call(
        trail_kernel,
        out_shape=jax.ShapeDtypeStruct(weight.shape, weight.dtype),
        grid_spec=pltpu.PrefetchScalarGridSpec(
            num_scalar_prefetch=1,
            grid=(rows // tile,),
            in_specs=[
                pl.BlockSpec((tile, pcols), lambda i, own: (i, 0)),
                pl.BlockSpec(
                    (pcols, width), lambda i, own: (0, 0), pipeline_mode=pl.Buffered(1)
                ),
                pl.BlockSpec((tile, width), lambda i, own: (i, 0)),
                pl.BlockSpec(
                    (tile, pcols), lambda i, own: (own[0] * jnp.minimum(i, split_at - 1), 0)
                ),
                pl.BlockSpec(
                    (tile, pcols), lambda i, own: (own[0] * jnp.maximum(i - split_at, 0), 0)
                ),
            ],
            out_specs=pl.BlockSpec((tile, width), lambda i, own: (i, 0)),
        ),
        compiler_params=pltpu.CompilerParams(vmem_limit_bytes=VMEM_BYTES),
        cost_estimate=pl.CostEstimate(
            flops=2 * rows * pcols * width,
            bytes_accessed=4 * rows * width + 2 * pcols * width,
            transcendentals=0,
        ),
        name="compensate_later",
    )(owner, errors, factor_low, weight, near, far)


def per_device(weight, factor, keep_mask, *, cols_n, rows_n):
    section = lax.axis_index("col")
    lane = lax.axis_index("row")
    depth = factor.shape[0]
    pcols = depth * rows_n
    rows = weight.shape[0]
    half = rows // 2
    to_core = [(r, rows_n + r) for r in range(rows_n)]

    def move(x, pairs):
        return lax.ppermute(x, ("col", "row"), pairs)

    own = factor[:, :pcols]
    panel = weight[:, :pcols]
    received = [own] + [
        move(own, [(r, (r + s) % rows_n) for r in range(rows_n)]) for s in range(1, rows_n)
    ]
    near_panel, far_panel = panel[:half], panel[half:]
    far_panel = move(far_panel, to_core)
    relayed = [move(x, to_core) for x in received]
    near_keep, far_keep = jnp.split(keep_mask, 2, axis=0)
    place = lane.astype(jnp.int32).reshape(1)

    factor_in, _ = lax.optimization_barrier((factor.astype(jnp.bfloat16), received[-1]))
    factor_low = lax.all_gather(factor_in, "row", axis=0, tiled=True)

    def near_case(near, far, mine, theirs):
        return prune(place, near, near_keep, *mine)

    def far_case(near, far, mine, theirs):
        return prune(place, far, far_keep, *theirs)

    def blank(near, far, mine, theirs):
        zeros = jnp.zeros((half, pcols), jnp.bfloat16)
        return zeros, zeros

    errors, kept = lax.switch(
        jnp.minimum(section, 2),
        [near_case, far_case, blank],
        near_panel,
        far_panel,
        received,
        relayed,
    )
    far_kept = move(kept, [(rows_n + r, r) for r in range(rows_n)])
    arrived = spread(errors, cols_n)
    owner = (section == 0).astype(jnp.int32).reshape(1)
    return trail(owner, arrived, factor_low, weight, kept, far_kept)


def solution(mesh):
    in_specs = (P("row", "col"), P("row", "col"), P("row", None))
    out_specs = P("row", "col")
    return jax.shard_map(
        partial(per_device, cols_n=mesh.shape["col"], rows_n=mesh.shape["row"]),
        mesh=mesh,
        in_specs=in_specs,
        out_specs=out_specs,
        check_vma=False,
    )
```

```python
from functools import partial

import jax
import jax.numpy as jnp
from jax import lax
from jax.experimental import pallas as pl
from jax.experimental.pallas import tpu as pltpu
from jax.sharding import PartitionSpec as P

BLK = 128
SUP = 256
VMEM_BYTES = 60 * 1024 * 1024


def split(x):
    high = x.astype(jnp.bfloat16)
    low = (x - high.astype(jnp.float32)).astype(jnp.bfloat16)
    return high, low


def mul(a, b):
    return jnp.dot(a, b, preferred_element_type=jnp.float32)


def mul3(a, b):
    a_high, a_low = split(a)
    b_high, b_low = split(b)
    return mul(a_high, b_high) + (mul(a_high, b_low) + mul(a_low, b_high))


def prune_kernel(lanes, lane_ref, keep_ref, w_ref, *refs):
    pieces = refs[:lanes]
    e_ref, kept_ref, f_high, band, blocks, inv, inv_high, inv_low, e_low, sems = refs[lanes:]
    chunk, pcols = w_ref.shape
    depth = pcols // lanes
    supers = inv.shape[0]
    row_id = lax.broadcasted_iota(jnp.int32, (SUP, SUP), 0)
    col_id = lax.broadcasted_iota(jnp.int32, (SUP, SUP), 1)

    @pl.when(pl.program_id(0) == 0)
    def _():
        copies = []
        for s in range(lanes):
            place = lax.rem(lane_ref[0] + lanes - s, lanes)
            rows = pl.ds(pl.multiple_of(place * depth, 16), depth)
            copies.append(
                pltpu.make_async_copy(pieces[s].at[:, :pcols], f_high.at[rows], sems.at[2 * s])
            )
            copies.append(
                pltpu.make_async_copy(pieces[s].at[:, pcols:], band.at[rows], sems.at[2 * s + 1])
            )
        for copy in copies:
            copy.start()
        for copy in copies:
            copy.wait()
        eye = row_id == col_id
        pair = (row_id // 2 == col_id // 2) & (row_id < col_id)
        for s in range(supers):
            lo = s * SUP
            width = min(SUP, pcols - lo)
            if width < SUP:
                blocks[s] = jnp.where(eye, 1.0, 0.0)
            shift = lo - min(lo, pcols - SUP)
            blocks[s, :width, :width] = f_high[lo : lo + width, lo : lo + width].astype(
                jnp.float32
            ) + band[lo : lo + width, shift : shift + width].astype(jnp.float32)
            block = blocks[s]
            diagonal = jnp.where(eye, block, 0.0)
            per_row = 1.0 / jnp.sum(diagonal, axis=1, keepdims=True)
            per_col = 1.0 / jnp.sum(diagonal, axis=0, keepdims=True)
            inv[s] = jnp.where(
                eye, per_row, jnp.where(pair, -(block * per_row) * per_col, 0.0)
            )

        def level(bit, carry):
            mask = (
                ((row_id >> (bit + 1)) == (col_id >> (bit + 1)))
                & (((row_id >> bit) & 1) == 0)
                & (((col_id >> bit) & 1) == 1)
            )
            for s in range(supers):
                x = inv[s]
                inv[s] = x - mul3(mul3(x, jnp.where(mask, blocks[s], 0.0)), x)
            return carry

        lax.fori_loop(1, SUP.bit_length() - 1, level, 0)
        for s in range(supers):
            high_part, low_part = split(inv[s])
            inv_high[s] = high_part
            inv_low[s] = low_part

    row_blocks = chunk // BLK
    base = pl.program_id(0) * row_blocks
    for s in range(supers):
        lo = s * SUP
        width = min(SUP, pcols - lo)
        cols = slice(lo, lo + width)
        current = w_ref[:, cols].astype(jnp.float32)
        if lo:
            head = e_ref[:, :lo]
            current = current - (
                mul(head, f_high[:lo, cols]) + mul(e_low[:, :lo], f_high[:lo, cols])
            )
        drop_rows = []
        for g in range(row_blocks):
            parts = []
            for b in range(lo // BLK, (lo + width) // BLK):
                kept_here = keep_ref[base + g, b].astype(jnp.float32)
                parts.append(jnp.full((BLK, BLK), 1.0 - kept_here, jnp.float32))
            drop_rows.append(parts[0] if len(parts) == 1 else jnp.concatenate(parts, axis=1))
        drop = jnp.concatenate(drop_rows, axis=0)
        c_high, c_low = split(jnp.where(drop > 0.5, current, 0.0))
        i_high = inv_high[s, :width, :width]
        solved = mul(c_high, i_high) + (
            mul(c_high, inv_low[s, :width, :width]) + mul(c_low, i_high)
        )
        high_part, low_part = split(jnp.where(drop > 0.5, solved, 0.0))
        e_ref[:, cols] = high_part
        e_low[:, cols] = low_part
        first = slice(lo, lo + BLK)
        kept_ref[:, first] = jnp.where(drop[:, :BLK] > 0.5, 0.0, current[:, :BLK]).astype(
            jnp.bfloat16
        )
        if width > BLK:
            second = slice(lo + BLK, lo + width)
            c_high, c_low = high_part[:, :BLK], low_part[:, :BLK]
            inner = mul(c_high, f_high[first, second]) + (
                mul(c_high, band[first, BLK:]) + mul(c_low, f_high[first, second])
            )
            kept_ref[:, second] = jnp.where(
                drop[:, BLK:] > 0.5, 0.0, current[:, BLK:] - inner
            ).astype(jnp.bfloat16)


def prune(lane, panel, keep_rows, *pieces):
    rows = keep_rows.shape[0] * BLK
    pcols = keep_rows.shape[1] * BLK
    chunk = min(rows, 512)
    supers = pl.cdiv(pcols, SUP)
    lanes = len(pieces)
    row_spec = pl.BlockSpec((chunk, pcols), lambda i: (i, 0))
    out = jax.ShapeDtypeStruct((rows, pcols), jnp.bfloat16)
    return pl.pallas_call(
        partial(prune_kernel, lanes),
        grid=(rows // chunk,),
        out_shape=(out, out),
        in_specs=[
            pl.BlockSpec(memory_space=pltpu.SMEM),
            pl.BlockSpec(memory_space=pltpu.SMEM),
            row_spec,
        ]
        + [pl.BlockSpec(memory_space=pl.ANY)] * lanes,
        out_specs=(row_spec, row_spec),
        scratch_shapes=[
            pltpu.VMEM((pcols, pcols), jnp.bfloat16),
            pltpu.VMEM((pcols, SUP), jnp.bfloat16),
            pltpu.VMEM((supers, SUP, SUP), jnp.float32),
            pltpu.VMEM((supers, SUP, SUP), jnp.float32),
            pltpu.VMEM((supers, SUP, SUP), jnp.bfloat16),
            pltpu.VMEM((supers, SUP, SUP), jnp.bfloat16),
            pltpu.VMEM((chunk, pcols), jnp.bfloat16),
            pltpu.SemaphoreType.DMA((2 * lanes,)),
        ],
        compiler_params=pltpu.CompilerParams(vmem_limit_bytes=VMEM_BYTES),
        cost_estimate=pl.CostEstimate(
            flops=6 * rows * pcols * pcols,
            bytes_accessed=6 * rows * pcols + 4 * pcols * pcols,
            transcendentals=0,
        ),
        name="prune_panel",
    )(lane, keep_rows, panel, *pieces)


def spread_kernel(
    chips, pieces, mine_ref, kept_ref, all_ref, far_ref, out_send, out_recv, sib_send, sib_recv, kept_sems
):
    index = lax.axis_index("col")
    core = index % 2
    chip = index // 2
    odd = chip % 2
    place = odd * ((chip + 1) // 2) + (1 - odd) * ((chips - chip // 2) % chips)

    def chip_at(p):
        upper = (p + chips // 2 - 1) // chips
        return (1 - upper) * (2 * p - 1) + upper * (2 * (chips - p)) + (chips - p) // chips

    step = (1 - core) * place + core * ((chips - place) % chips)
    way = 1 - 2 * core
    after = chip_at((place + way + chips) % chips) * 2 + core
    before = chip_at((place - way + chips) % chips) * 2 + core
    sibling = chip * 2 + 1 - core
    half = mine_ref.shape[0]
    size = half // pieces

    def signal(where, sem):
        pl.semaphore_signal(sem, inc=1, device_id={"col": where}, device_id_type=pl.DeviceIdType.MESH)

    barrier = pltpu.get_barrier_semaphore()
    signal(sibling, barrier)

    @pl.when(step > 0)
    def _():
        signal(before, barrier)

    @pl.when(step < chips - 1)
    def _():
        pl.semaphore_wait(barrier, 2)

    @pl.when(step == chips - 1)
    def _():
        pl.semaphore_wait(barrier, 1)

    def piece(which, t):
        return all_ref.at[pl.ds(pl.multiple_of(which * half + t * size, 16), size)]

    def forward(t):
        return pltpu.make_async_remote_copy(
            src_ref=piece(core, t),
            dst_ref=piece(core, t),
            send_sem=out_send.at[t],
            recv_sem=out_recv.at[t],
            device_id={"col": after},
            device_id_type=pl.DeviceIdType.MESH,
        )

    def across(t, which):
        return pltpu.make_async_remote_copy(
            src_ref=piece(which, t),
            dst_ref=piece(which, t),
            send_sem=sib_send.at[t],
            recv_sem=sib_recv.at[t],
            device_id={"col": sibling},
            device_id_type=pl.DeviceIdType.MESH,
        )

    def pass_on(t, carry):
        @pl.when(step == 0)
        def _():
            here = pl.ds(pl.multiple_of(core * half + t * size, 16), size)
            all_ref[here] = mine_ref[pl.ds(pl.multiple_of(t * size, 16), size)]

        @pl.when(step > 0)
        def _():
            forward(t).wait_recv()

        @pl.when(step < chips - 1)
        def _():
            forward(t).start()

        across(t, core).start()
        return carry

    lax.fori_loop(0, pieces, pass_on, 0)
    kept_copy = pltpu.make_async_remote_copy(
        src_ref=kept_ref,
        dst_ref=far_ref,
        send_sem=kept_sems.at[0],
        recv_sem=kept_sems.at[1],
        device_id={"col": sibling},
        device_id_type=pl.DeviceIdType.MESH,
    )

    @pl.when(index == 1)
    def _():
        kept_copy.start()

    def finish(t, carry):
        @pl.when(step < chips - 1)
        def _():
            forward(t).wait_send()

        across(t, core).wait_send()
        across(t, 1 - core).wait_recv()
        return carry

    lax.fori_loop(0, pieces, finish, 0)

    @pl.when(index == 1)
    def _():
        kept_copy.wait_send()

    @pl.when(index == 0)
    def _():
        kept_copy.wait_recv()


def spread(errors, kept, devices):
    half, pcols = errors.shape
    pieces = half // 64
    return pl.pallas_call(
        partial(spread_kernel, devices // 2, pieces),
        out_shape=(
            jax.ShapeDtypeStruct((2 * half, pcols), jnp.bfloat16),
            jax.ShapeDtypeStruct((half, pcols), jnp.bfloat16),
        ),
        in_specs=[pl.BlockSpec(memory_space=pltpu.VMEM)] * 2,
        out_specs=(pl.BlockSpec(memory_space=pltpu.VMEM),) * 2,
        scratch_shapes=[pltpu.SemaphoreType.DMA((pieces,))] * 4 + [pltpu.SemaphoreType.DMA((2,))],
        compiler_params=pltpu.CompilerParams(
            collective_id=0, has_side_effects=True, vmem_limit_bytes=VMEM_BYTES
        ),
        cost_estimate=pl.CostEstimate(
            flops=0, bytes_accessed=16 * half * pcols, transcendentals=0
        ),
        name="spread_errors",
    )(errors, kept)


def trail_kernel(owner_ref, e_ref, f_ref, w_ref, near_ref, far_ref, out_ref):
    pcols = e_ref.shape[1]
    width = w_ref.shape[1]
    owner = owner_ref[0] == 1

    def compensated(cols):
        product = mul(e_ref[...], f_ref[:, cols])
        return (w_ref[:, cols].astype(jnp.float32) - product).astype(jnp.bfloat16)

    first = pl.program_id(0) < pl.num_programs(0) // 2

    @pl.when(owner & first)
    def _():
        out_ref[:, :pcols] = near_ref[...]

    @pl.when(owner & jnp.logical_not(first))
    def _():
        out_ref[:, :pcols] = far_ref[...]

    @pl.when(jnp.logical_not(owner))
    def _():
        for low in range(0, pcols, SUP):
            cols = slice(low, min(low + SUP, pcols))
            out_ref[:, cols] = compensated(cols)

    for low in range(pcols, width, SUP):
        cols = slice(low, min(low + SUP, width))
        out_ref[:, cols] = compensated(cols)


def trail(owner, errors, factor_low, weight, near, far):
    rows, width = weight.shape
    pcols = errors.shape[1]
    tile = min(rows // 2, 512)
    split_at = rows // 2 // tile
    return pl.pallas_call(
        trail_kernel,
        out_shape=jax.ShapeDtypeStruct(weight.shape, weight.dtype),
        grid_spec=pltpu.PrefetchScalarGridSpec(
            num_scalar_prefetch=1,
            grid=(rows // tile,),
            in_specs=[
                pl.BlockSpec((tile, pcols), lambda i, own: (i, 0)),
                pl.BlockSpec(
                    (pcols, width), lambda i, own: (0, 0), pipeline_mode=pl.Buffered(1)
                ),
                pl.BlockSpec((tile, width), lambda i, own: (i, 0)),
                pl.BlockSpec(
                    (tile, pcols), lambda i, own: (own[0] * jnp.minimum(i, split_at - 1), 0)
                ),
                pl.BlockSpec(
                    (tile, pcols), lambda i, own: (own[0] * jnp.maximum(i - split_at, 0), 0)
                ),
            ],
            out_specs=pl.BlockSpec((tile, width), lambda i, own: (i, 0)),
        ),
        compiler_params=pltpu.CompilerParams(vmem_limit_bytes=VMEM_BYTES),
        cost_estimate=pl.CostEstimate(
            flops=2 * rows * pcols * width,
            bytes_accessed=4 * rows * width + 2 * pcols * width,
            transcendentals=0,
        ),
        name="compensate_later",
    )(owner, errors, factor_low, weight, near, far)


def per_device(weight, factor, keep_mask, *, cols_n, rows_n):
    section = lax.axis_index("col")
    lane = lax.axis_index("row")
    depth = factor.shape[0]
    pcols = depth * rows_n
    rows = weight.shape[0]
    half = rows // 2
    to_core = [(r, rows_n + r) for r in range(rows_n)]

    def move(x, pairs):
        return lax.ppermute(x, ("col", "row"), pairs)

    own = factor[:, :pcols]
    rounded = lax.reduce_precision(own, 8, 7)
    remainder = (own - rounded).astype(jnp.bfloat16)
    super_of = ((lane * depth + jnp.arange(depth, dtype=jnp.int32)) // SUP)[:, None]
    band = remainder[:, :SUP]
    for low in range(SUP, pcols, SUP):
        start = min(low, pcols - SUP)
        band = jnp.where(super_of == low // SUP, remainder[:, start : start + SUP], band)
    own = jnp.concatenate([rounded.astype(jnp.bfloat16), band], axis=1)
    received = [own] + [
        move(own, [(r, (r + s) % rows_n) for r in range(rows_n)]) for s in range(1, rows_n)
    ]
    far_panel = move(weight[half:, :pcols], to_core)
    relayed = [move(x, to_core) for x in received]
    near_keep, far_keep = jnp.split(keep_mask, 2, axis=0)
    place = lane.astype(jnp.int32).reshape(1)

    factor_in, _ = lax.optimization_barrier((factor.astype(jnp.bfloat16), received[-1]))
    factor_low = lax.all_gather(factor_in, "row", axis=0, tiled=True)

    def near_case(near, far, mine, theirs):
        return prune(place, near, near_keep, *mine)

    def far_case(near, far, mine, theirs):
        return prune(place, far, far_keep, *theirs)

    def blank(near, far, mine, theirs):
        zeros = jnp.zeros((half, pcols), jnp.bfloat16)
        return zeros, zeros

    errors, kept = lax.switch(
        jnp.minimum(section, 2),
        [near_case, far_case, blank],
        weight,
        far_panel,
        received,
        relayed,
    )
    arrived, far_kept = spread(errors, kept, cols_n)
    owner = (section == 0).astype(jnp.int32).reshape(1)
    return trail(owner, arrived, factor_low, weight, kept, far_kept)


def solution(mesh):
    in_specs = (P("row", "col"), P("row", "col"), P("row", None))
    out_specs = P("row", "col")
    return jax.shard_map(
        partial(per_device, cols_n=mesh.shape["col"], rows_n=mesh.shape["row"]),
        mesh=mesh,
        in_specs=in_specs,
        out_specs=out_specs,
        check_vma=False,
    )
```
